32 devices in a mesh: replica: 8 (over y, x, core), fsdp: 4 (over z).
Axes of the slice: x: 2, y: 2, z: 4, core: 2. Of those that a mesh axis runs over, the one named last changes fastest.
Arguments:
- tokens: bfloat16 [4096, 4096], P(('replica', 'fsdp')), may hold values from -6 to 6
- out_grads: bfloat16 [4096, 14336], P(('replica', 'fsdp')), may hold values from -0.25 to 0.25
- block_ids: int32 [4], replicated, may hold values from 0 to 55, as said below
- left_basis: bfloat16 [8, 4, 1024, 1024], P('replica', 'fsdp'), may hold values from -0.1875 to 0.1875
- right_basis: bfloat16 [8, 4, 1024, 1024], P('replica', 'fsdp'), may hold values from -0.1875 to 0.1875
- first_moment: bfloat16 [8, 4, 1024, 1024], P('replica', 'fsdp'), may hold values from -3 to 3
- second_moment: bfloat16 [8, 4, 1024, 1024], P('replica', 'fsdp'), may hold values from 0.0099487305 to 1
- outer_params: float32 [512, 8192], P('fsdp'), may hold values from -6 to 6
- outer_momentum: float32 [512, 8192], P('fsdp'), may hold values from -3 to 3
- snapshot: bfloat16 [8, 512, 8192], P('replica', 'fsdp'), may hold values from -6 to 6
- local_params: bfloat16 [8, 512, 8192], P('replica', 'fsdp'), may hold values from -6 to 6
- due_rows: int32 [512], P('fsdp'), may hold values 0 or 1
Outputs:
- update: bfloat16 [8, 4, 1024, 1024], P('replica', 'fsdp')
- first_next: bfloat16 [8, 4, 1024, 1024], P('replica', 'fsdp')
- second_next: bfloat16 [8, 4, 1024, 1024], P('replica', 'fsdp')
- outer_next: float32 [512, 8192], P('fsdp')
- momentum_next: float32 [512, 8192], P('fsdp')
- local_next: bfloat16 [8, 512, 8192], P('replica', 'fsdp')
The draws below stay inside these ranges and needn't reach their ends.
Inputs may be any that keep to these rules, and one draw needn't show every extreme that they name: `block_ids`: 4 different block numbers of the window; slot s belongs to fsdp index s.
All inputs are finite; a program needn't handle non-finite values. No bound on the sum of `due_rows` on one device may be relied on, other than what follows from the above.
Results may differ from the reference program's by a relative error of at most 0.022.
Values may be sent and summed in bfloat16 or wider, within the bound.
A program may use at most 192 MiB of HBM per device.

```python
import math
import jax
import jax.numpy as jnp
from jax import lax

D = 8192
DW = 4096
FW = 14336
BLOCK = 1024
TOK_DEV = 128
GRID = 56
NBLK = 4
TOKENS = 4096
FRAG_ROWS = 512
REPLICAS = 8
N_REPLICA = 8
N_FSDP = 4


def draw_block_ids(key, part):
    key = jax.random.fold_in(key, 11)
    first_key, second_key = jax.random.split(key)
    middle = jax.random.permutation(first_key, GRID - 2) + 1
    chosen = jnp.concatenate([jnp.array([0, GRID - 1], jnp.int32), middle[:NBLK - 2].astype(jnp.int32)])
    return jax.random.permutation(second_key, chosen).astype(jnp.int32)


def with_ends(entries, key, smallest, largest):
    longest = entries.shape.index(max(entries.shape))
    spots = []
    for shift in (0, 1):
        where = [jax.random.randint(jax.random.fold_in(key, axis), (), 0, length) for axis, length in enumerate(entries.shape)]
        where[longest] = (where[longest] + shift) % entries.shape[longest]
        spots.append(tuple(where))
    return entries.at[spots[0]].set(smallest).at[spots[1]].set(largest)


def steps_of(key, extent, shards, low, high):
    gain = 1.0
    for dim, blocks in shards:
        steps = jax.random.uniform(jax.random.fold_in(jax.random.fold_in(key, 6), dim), (blocks,), jnp.float32, low / len(shards), high / len(shards))
        gain = gain * jnp.repeat(jnp.exp(steps), extent[dim] // blocks).reshape((-1,) + (1,) * (len(extent) - 1 - dim))
    return gain


def scatter_about(stream_key, shape, width, most, cuts=(), kind=jnp.bfloat16):
    loudness = steps_of(stream_key, shape, cuts, -0.22, 0.18) if cuts else 1.0
    values = jax.random.normal(stream_key, shape, jnp.float32) * width * loudness
    return jnp.minimum(jnp.maximum(values, -most), most).astype(kind)


def setup_inputs(seed: int = 0) -> dict:
    splits = jax.random.split(jax.random.key(seed), 13)
    tokens = scatter_about(splits[0], (TOKENS, DW), 1.0, 6.0, ((0, 32),))
    out_grads = scatter_about(splits[1], (TOKENS, FW), (TOK_DEV * N_FSDP) ** -0.5, 0.25, ((0, 32),))
    block_ids = draw_block_ids(jax.random.fold_in(splits[12], 71), 0)
    left_basis = scatter_about(splits[3], (REPLICAS, NBLK, BLOCK, BLOCK), BLOCK ** -0.5, 0.1875, ((0, 8), (1, 4)))
    right_basis = scatter_about(splits[4], (REPLICAS, NBLK, BLOCK, BLOCK), BLOCK ** -0.5, 0.1875, ((0, 8), (1, 4)))
    first_moment = scatter_about(splits[5], (REPLICAS, NBLK, BLOCK, BLOCK), 0.5, 3.0, ((0, 8), (1, 4)))
    second_moment = jnp.clip(jnp.exp(math.log(1.0) - 4.61031033 * jax.random.uniform(splits[6], (REPLICAS, NBLK, BLOCK, BLOCK), jnp.float32) ** steps_of(splits[6], (REPLICAS, NBLK, BLOCK, BLOCK), ((0, 8), (1, 4)), -0.2, 0.2)), 0.0099487305, 1.0).astype(jnp.bfloat16)
    outer_params = scatter_about(splits[7], (FRAG_ROWS, D), 1.0, 6.0, ((0, 4),), jnp.float32)
    outer_momentum = scatter_about(splits[8], (FRAG_ROWS, D), 0.5, 3.0, ((0, 4),), jnp.float32)
    snapshot = scatter_about(splits[9], (REPLICAS, FRAG_ROWS, D), 1.0, 6.0, ((0, 8), (1, 4)))
    local_params = scatter_about(splits[10], (REPLICAS, FRAG_ROWS, D), 1.0, 6.0, ((0, 8), (1, 4)))
    due_rows = with_ends((jax.random.randint(splits[11], (FRAG_ROWS,), 0, 2) < 1).astype(jnp.int32), jax.random.fold_in(splits[11], 1), 0, 1)
    return dict(tokens=tokens, out_grads=out_grads, block_ids=block_ids, left_basis=left_basis, right_basis=right_basis, first_moment=first_moment, second_moment=second_moment, outer_params=outer_params, outer_momentum=outer_momentum, snapshot=snapshot, local_params=local_params, due_rows=due_rows)


def soap_block(grad, left, right, first, second):
    half = jnp.dot(left.T, grad, preferred_element_type=jnp.float32).astype(jnp.bfloat16)
    rotated = jnp.dot(half, right, preferred_element_type=jnp.float32)
    moment_one = 0.95 * first.astype(jnp.float32) + 0.05 * rotated
    moment_two = 0.95 * second.astype(jnp.float32) + 0.05 * rotated * rotated
    correct = 1.0 - 0.95 ** 10
    direction = (moment_one / correct / (jnp.sqrt(moment_two / correct) + 1e-08)).astype(jnp.bfloat16)
    back = jnp.dot(left, direction, preferred_element_type=jnp.float32).astype(jnp.bfloat16)
    update = jnp.dot(back, right.T, preferred_element_type=jnp.float32).astype(jnp.bfloat16)
    return (update, moment_one.astype(jnp.bfloat16), moment_two.astype(jnp.bfloat16))

def reference(tokens, out_grads, block_ids, left_basis, right_basis, first_moment, second_moment, outer_params, outer_momentum, snapshot, local_params, due_rows):
    columns = FW // BLOCK
    inputs = tokens.reshape(N_REPLICA, N_FSDP, TOK_DEV, DW)
    grads_out = out_grads.reshape(N_REPLICA, N_FSDP, TOK_DEV, FW)

    def one_replica(items):
        xin, dout, lefts, rights, firsts, seconds = items

        def one_block(entry):
            block, left, right, first, second = entry
            row_start = block // columns * BLOCK
            col_start = block % columns * BLOCK
            xcols = lax.dynamic_slice_in_dim(xin, row_start, BLOCK, 2).astype(jnp.float32)
            dcols = lax.dynamic_slice_in_dim(dout, col_start, BLOCK, 2).astype(jnp.float32)
            parts = jnp.einsum('fti,ftj->fij', xcols, dcols)
            parts = lax.optimization_barrier(parts.astype(jnp.bfloat16)).astype(jnp.float32)
            grad = lax.optimization_barrier(jnp.sum(parts, axis=0)).astype(jnp.bfloat16)
            return soap_block(grad, left, right, first, second)
        return lax.map(one_block, (block_ids, lefts, rights, firsts, seconds))
    update, first_next, second_next = lax.map(one_replica, (inputs, grads_out, left_basis, right_basis, first_moment, second_moment))
    snap = snapshot.astype(jnp.float32)
    pseudo = lax.optimization_barrier(jnp.sum(outer_params[None] - snap, axis=0)) / N_REPLICA
    moment = 0.9 * outer_momentum + pseudo
    stepped = outer_params - 0.7 * (pseudo + 0.9 * moment)
    due = (due_rows == 1)[:, None]
    outer_next = jnp.where(due, stepped, outer_params)
    momentum_next = jnp.where(due, moment, outer_momentum)
    merged = (stepped[None] + (local_params.astype(jnp.float32) - snap)).astype(jnp.bfloat16)
    local_next = jnp.where(due[None], merged, local_params)
    return (update, first_next, second_next, outer_next, momentum_next, local_next)
```

```python
import jax
import jax.numpy as jnp
from jax import lax
from jax.sharding import PartitionSpec as P


def per_device(
    tokens,
    out_grads,
    block_ids,
    left_basis,
    right_basis,
    first_moment,
    second_moment,
    outer_params,
    outer_momentum,
    snapshot,
    local_params,
    due_rows,
):
    width = left_basis.shape[-1]
    columns = out_grads.shape[1] // width
    n = lax.axis_size("fsdp")
    me = lax.axis_index("fsdp")
    left = left_basis[0, 0]
    right = right_basis[0, 0]

    def block_cols(slot):
        block = block_ids[slot]
        xcols = lax.dynamic_slice_in_dim(tokens, block // columns * width, width, 1)
        dcols = lax.dynamic_slice_in_dim(out_grads, block % columns * width, width, 1)
        return jnp.stack([xcols, dcols])

    arrived = [block_cols(me)]
    for shift in range(1, n):
        arrived.append(
            lax.ppermute(
                block_cols((me + shift) % n),
                "fsdp",
                [(i, (i + shift) % n) for i in range(n)],
            )
        )
    snap_sum = lax.psum(snapshot[0], "replica").astype(jnp.float32)

    xl = [
        jnp.dot(part[0], left, preferred_element_type=jnp.float32).astype(jnp.bfloat16)
        for part in arrived
    ]
    dr = [
        jnp.dot(part[1], right, preferred_element_type=jnp.float32).astype(jnp.bfloat16)
        for part in arrived
    ]
    rotated = lax.dot_general(
        jnp.concatenate(xl),
        jnp.concatenate(dr),
        (((0,), (0,)), ((), ())),
        preferred_element_type=jnp.float32,
    )
    moment_one = 0.95 * first_moment[0, 0].astype(jnp.float32) + 0.05 * rotated
    moment_two = 0.95 * second_moment[0, 0].astype(jnp.float32) + 0.05 * rotated * rotated
    correct = 1.0 - 0.95**10
    direction = (moment_one / correct / (jnp.sqrt(moment_two / correct) + 1e-08)).astype(
        jnp.bfloat16
    )
    back = jnp.dot(left, direction, preferred_element_type=jnp.float32).astype(jnp.bfloat16)
    update = lax.dot_general(
        back, right, (((1,), (1,)), ((), ())), preferred_element_type=jnp.float32
    ).astype(jnp.bfloat16)

    snap = snapshot[0].astype(jnp.float32)
    pseudo = outer_params - snap_sum / lax.axis_size("replica")
    moment = 0.9 * outer_momentum + pseudo
    stepped = outer_params - 0.7 * (pseudo + 0.9 * moment)
    due = (due_rows == 1)[:, None]
    outer_next = jnp.where(due, stepped, outer_params)
    momentum_next = jnp.where(due, moment, outer_momentum)
    merged = (stepped + (local_params[0].astype(jnp.float32) - snap)).astype(jnp.bfloat16)
    local_next = jnp.where(due, merged, local_params[0])
    return (
        update[None, None],
        moment_one.astype(jnp.bfloat16)[None, None],
        moment_two.astype(jnp.bfloat16)[None, None],
        outer_next,
        momentum_next,
        local_next[None],
    )


def solution(mesh):
    return jax.shard_map(
        per_device,
        mesh=mesh,
        in_specs=(
            P(("replica", "fsdp"), None),
            P(("replica", "fsdp"), None),
            P(),
            P("replica", "fsdp", None, None),
            P("replica", "fsdp", None, None),
            P("replica", "fsdp", None, None),
            P("replica", "fsdp", None, None),
            P("fsdp", None),
            P("fsdp", None),
            P("replica", "fsdp", None),
            P("replica", "fsdp", None),
            P("fsdp"),
        ),
        out_specs=(
            P("replica", "fsdp", None, None),
            P("replica", "fsdp", None, None),
            P("replica", "fsdp", None, None),
            P("fsdp", None),
            P("fsdp", None),
            P("replica", "fsdp", None),
        ),
        check_vma=False,
    )
```

```python
import functools

import jax
import jax.numpy as jnp
from jax import lax
from jax.experimental import pallas as pl
from jax.experimental.pallas import tpu as pltpu
from jax.sharding import PartitionSpec as P

MIB = 1 << 20
CORES = 2
CORRECT = 1.0 - 0.95**10


def any_spec():
    return pl.BlockSpec(memory_space=pl.ANY)


def vmem_spec():
    return pl.BlockSpec(memory_space=pltpu.VMEM)


def gather_kernel(n, width, columns, order, ids, tokens, out_grads, *refs):
    outs, sems = refs[:n], refs[n]
    me = lax.axis_index("fsdp")
    copies = []
    for k, shift in enumerate(order):
        block = ids[lax.rem(me + shift, n)]
        row = pl.multiple_of(block // columns * width, width)
        col = pl.multiple_of(lax.rem(block, columns) * width, width)
        copies.append(
            pltpu.make_async_copy(tokens.at[:, pl.ds(row, width)], outs[k].at[0], sems.at[0, k])
        )
        copies.append(
            pltpu.make_async_copy(out_grads.at[:, pl.ds(col, width)], outs[k].at[1], sems.at[1, k])
        )
    for copy in copies:
        copy.start()
    for copy in copies:
        copy.wait()


def gather(tokens, out_grads, block_ids, width, n, order):
    rows = tokens.shape[0]
    return pl.pallas_call(
        functools.partial(gather_kernel, n, width, out_grads.shape[1] // width, order),
        out_shape=[jax.ShapeDtypeStruct((2, rows, width), tokens.dtype)] * n,
        in_specs=[pl.BlockSpec(memory_space=pltpu.SMEM), any_spec(), any_spec()],
        out_specs=[any_spec()] * n,
        scratch_shapes=[pltpu.SemaphoreType.DMA((2, n))],
        compiler_params=pltpu.CompilerParams(vmem_limit_bytes=4 * MIB),
        cost_estimate=pl.CostEstimate(flops=0, bytes_accessed=16 * n * rows * width, transcendentals=0),
        name="gather_slots",
    )(block_ids, tokens, out_grads)


def sum_kernel(
    chips, own, out, sib, part, inbox, s1, r1, s2, r2, s3, r3, s4, r4
):
    me = lax.axis_index("replica")
    chip, core = me // CORES, lax.rem(me, CORES)
    half, wide = own.shape[0] // CORES, own.shape[1] // chips
    other = 1 - core
    sibling = {"replica": chip * CORES + other}

    def peer(k):
        return lax.rem(chip + k, chips)

    def rows(c):
        return pl.ds(pl.multiple_of(c * half, half), half)

    def cols(c):
        return pl.ds(pl.multiple_of(c * wide, wide), wide)

    def to(k):
        return {"replica": peer(k) * CORES + core}

    barrier = pltpu.get_barrier_semaphore()
    pl.semaphore_signal(barrier, inc=1, device_id=sibling, device_id_type=pl.DeviceIdType.MESH)
    for k in range(1, chips):
        pl.semaphore_signal(barrier, inc=1, device_id=to(k), device_id_type=pl.DeviceIdType.MESH)
    pl.semaphore_wait(barrier, chips)

    turns = list(range(1, chips)) + [0]
    remote = functools.partial(
        pltpu.make_async_remote_copy, device_id_type=pl.DeviceIdType.MESH
    )
    first = {
        k: remote(own.at[rows(other), cols(peer(k))], sib.at[k], s1.at[k], r1.at[k], device_id=sibling)
        for k in turns
    }
    for k in turns:
        first[k].start()
    second = {}
    for k in turns:
        first[k].wait_recv()
        pair = own[rows(core), cols(peer(k))].astype(jnp.float32) + sib[k].astype(jnp.float32)
        if k:
            part[k] = pair.astype(part.dtype)
            second[k] = remote(part.at[k], inbox.at[k], s2.at[k], r2.at[k], device_id=to(k))
            second[k].start()
        else:
            part[0] = pair.astype(part.dtype)
    for k in range(1, chips):
        second[k].wait_recv()
    total = part[0].astype(jnp.float32)
    for k in range(1, chips):
        total = total + inbox[k].astype(jnp.float32)
    out[rows(core), cols(chip)] = total.astype(out.dtype)

    mine = out.at[rows(core), cols(chip)]
    third = {}
    for k in range(1, chips):
        third[k] = remote(mine, mine, s3.at[k], r3.at[k], device_id=to(k))
        third[k].start()
    fourth = {0: remote(mine, mine, s4.at[0], r4.at[0], device_id=sibling)}
    fourth[0].start()
    for k in range(1, chips):
        third[k].wait_recv()
        landed = out.at[rows(core), cols(lax.rem(chip + chips - k, chips))]
        fourth[k] = remote(landed, landed, s4.at[k], r4.at[k], device_id=sibling)
        fourth[k].start()
    for k in range(chips):
        fourth[k].wait_recv()
        fourth[k].wait_send()
        first[k].wait_send()
        if k:
            second[k].wait_send()
            third[k].wait_send()


def replica_sum(snap, replicas):
    chips = replicas // CORES
    rows, cols = snap.shape
    piece = (chips, rows // CORES, cols // chips)
    dma = pltpu.SemaphoreType.DMA((chips,))
    return pl.pallas_call(
        functools.partial(sum_kernel, chips),
        out_shape=jax.ShapeDtypeStruct(snap.shape, snap.dtype),
        in_specs=[vmem_spec()],
        out_specs=vmem_spec(),
        scratch_shapes=[pltpu.VMEM(piece, snap.dtype)] * 3 + [dma] * 8,
        compiler_params=pltpu.CompilerParams(
            collective_id=0, has_side_effects=True, vmem_limit_bytes=16 * MIB
        ),
        cost_estimate=pl.CostEstimate(flops=0, bytes_accessed=48 * snap.size, transcendentals=0),
        name="replica_sum",
    )(snap)


def fragment_kernel(scale, total, outer, momentum, snap, local, due, outer_next, momentum_next, local_next):
    base, old = outer[...], momentum[...]
    pseudo = base - total[...].astype(jnp.float32) * scale
    moment = 0.9 * old + pseudo
    stepped = base - 0.7 * (pseudo + 0.9 * moment)
    keep = due[...] == 1
    outer_next[...] = jnp.where(keep, stepped, base)
    momentum_next[...] = jnp.where(keep, moment, old)
    here = local[...].astype(jnp.float32)
    merged = stepped + (here - snap[...].astype(jnp.float32))
    local_next[...] = jnp.where(keep, merged, here).astype(local_next.dtype)


def fragment(total, outer, momentum, snap, local, due, replicas):
    rows, cols = outer.shape
    step = 16
    spec = pl.BlockSpec((step, cols), lambda i: (i, 0))
    return pl.pallas_call(
        functools.partial(fragment_kernel, 1.0 / replicas),
        grid=(rows // step,),
        out_shape=[
            jax.ShapeDtypeStruct(outer.shape, outer.dtype),
            jax.ShapeDtypeStruct(outer.shape, outer.dtype),
            jax.ShapeDtypeStruct(local.shape, local.dtype),
        ],
        in_specs=[spec] * 5 + [pl.BlockSpec((step, 1), lambda i: (i, 0))],
        out_specs=[spec] * 3,
        compiler_params=pltpu.CompilerParams(vmem_limit_bytes=24 * MIB),
        cost_estimate=pl.CostEstimate(
            flops=12 * outer.size, bytes_accessed=24 * outer.size, transcendentals=0
        ),
        name="fragment_step",
    )(total, outer, momentum, snap, local, due.reshape(rows, 1))


def early_kernel(m, *refs):
    parts, left, right, xlt, dr = refs[:m], refs[m], refs[m + 1], refs[m + 2], refs[m + 3]
    rows = parts[0].shape[1]
    for k in range(m):
        span = slice(k * rows, (k + 1) * rows)
        xl = jnp.dot(parts[k][0], left[...], preferred_element_type=jnp.float32)
        xlt[:, span] = xl.T.astype(xlt.dtype)
        dr[span, :] = jnp.dot(
            parts[k][1], right[...], preferred_element_type=jnp.float32
        ).astype(dr.dtype)


def early(parts, left, right):
    m = len(parts)
    rows, width = parts[0].shape[1:]
    return pl.pallas_call(
        functools.partial(early_kernel, m),
        out_shape=[
            jax.ShapeDtypeStruct((width, m * rows), left.dtype),
            jax.ShapeDtypeStruct((m * rows, width), left.dtype),
        ],
        in_specs=[vmem_spec()] * (m + 2),
        out_specs=[vmem_spec()] * 2,
        compiler_params=pltpu.CompilerParams(vmem_limit_bytes=24 * MIB),
        cost_estimate=pl.CostEstimate(
            flops=4 * m * rows * width * width, bytes_accessed=8 * MIB, transcendentals=0
        ),
        name="early_products",
    )(*parts, left, right)


def tail_kernel(
    step, last, xlt_in, dr_in, left_in, right_in, first_in, second_in,
    update, first_next, second_next,
    tail, xlt, dr, left, right, first, second, first_out, second_out, back, up, sems, chunk_sems,
):
    width = left.shape[0]
    rows = tail.shape[1]
    done = dr_in.shape[0]
    chunks = [slice(k * step, (k + 1) * step) for k in range(width // step)]
    load = [
        pltpu.make_async_copy(last, tail, sems.at[0]),
        pltpu.make_async_copy(left_in, left, sems.at[1]),
        pltpu.make_async_copy(right_in, right, sems.at[2]),
        pltpu.make_async_copy(dr_in, dr.at[:done], sems.at[3]),
        pltpu.make_async_copy(xlt_in, xlt.at[:, :done], sems.at[4]),
    ]
    for copy in load:
        copy.start()
    firsts = [
        pltpu.make_async_copy(first_in.at[:, c], first.at[:, c], chunk_sems.at[0, k])
        for k, c in enumerate(chunks)
    ]
    seconds = [
        pltpu.make_async_copy(second_in.at[:, c], second.at[:, c], chunk_sems.at[1, k])
        for k, c in enumerate(chunks)
    ]
    for one, two in zip(firsts, seconds):
        one.start()
        two.start()
    load[0].wait()
    load[1].wait()
    xl = jnp.dot(tail[0], left[...], preferred_element_type=jnp.float32)
    xlt[:, done:] = xl.T.astype(xlt.dtype)
    load[2].wait()
    dr[done:, :] = jnp.dot(tail[1], right[...], preferred_element_type=jnp.float32).astype(dr.dtype)
    load[3].wait()
    load[4].wait()
    stores = []
    for k, c in enumerate(chunks):
        rotated = jnp.dot(xlt[...], dr[:, c], preferred_element_type=jnp.float32)
        firsts[k].wait()
        seconds[k].wait()
        one = 0.95 * first[:, c].astype(jnp.float32) + 0.05 * rotated
        two = 0.95 * second[:, c].astype(jnp.float32) + 0.05 * (rotated * rotated)
        first_out[:, c] = one.astype(first_out.dtype)
        second_out[:, c] = two.astype(second_out.dtype)
        stores.append(
            pltpu.make_async_copy(first_out.at[:, c], first_next.at[:, c], chunk_sems.at[2, k])
        )
        stores.append(
            pltpu.make_async_copy(second_out.at[:, c], second_next.at[:, c], chunk_sems.at[3, k])
        )
        stores[-2].start()
        stores[-1].start()
        scaled = CORRECT * two
        bottom = scaled * lax.rsqrt(scaled) + CORRECT * 1e-08
        guess = pl.reciprocal(bottom, approx=True)
        direction = (one * (guess * (2.0 - bottom * guess))).astype(jnp.bfloat16)
        back[:, c] = jnp.dot(left[...], direction, preferred_element_type=jnp.float32).astype(
            back.dtype
        )
    for k, c in enumerate(chunks):
        up[:, c] = lax.dot_general(
            back[...], right[c, :], (((1,), (1,)), ((), ())), preferred_element_type=jnp.float32
        ).astype(up.dtype)
        stores.append(pltpu.make_async_copy(up.at[:, c], update.at[:, c], chunk_sems.at[4, k]))
        stores[-1].start()
    for copy in stores:
        copy.wait()


def finish(last, xlt, dr, left, right, first, second):
    width = left.shape[0]
    rows = last.shape[1]
    tokens = dr.shape[0] + rows
    step = 256
    square = pltpu.VMEM((width, width), left.dtype)
    return pl.pallas_call(
        functools.partial(tail_kernel, step),
        out_shape=[jax.ShapeDtypeStruct((width, width), left.dtype)] * 3,
        in_specs=[any_spec()] * 7,
        out_specs=[any_spec()] * 3,
        scratch_shapes=[
            pltpu.VMEM(last.shape, last.dtype),
            pltpu.VMEM((width, tokens), left.dtype),
            pltpu.VMEM((tokens, width), left.dtype),
        ]
        + [square] * 8
        + [pltpu.SemaphoreType.DMA((5,)), pltpu.SemaphoreType.DMA((5, width // step))],
        compiler_params=pltpu.CompilerParams(vmem_limit_bytes=40 * MIB),
        cost_estimate=pl.CostEstimate(
            flops=6 * width**3, bytes_accessed=14 * MIB, transcendentals=2 * width * width
        ),
        name="soap_tail",
    )(last, xlt, dr, left, right, first, second)


def per_device(
    tokens,
    out_grads,
    block_ids,
    left_basis,
    right_basis,
    first_moment,
    second_moment,
    outer_params,
    outer_momentum,
    snapshot,
    local_params,
    due_rows,
):
    n = lax.axis_size("fsdp")
    replicas = lax.axis_size("replica")
    left, right = left_basis[0, 0], right_basis[0, 0]
    order = [0] + sorted(range(1, n), key=lambda s: abs(2 * s - n))
    sent = gather(tokens, out_grads, block_ids, left.shape[-1], n, order)
    parts = [sent[0]]
    for k in range(1, n):
        pairs = [(i, (i + order[k]) % n) for i in range(n)]
        parts.append(lax.ppermute(sent[k], "fsdp", pairs))
    total = replica_sum(snapshot[0], replicas)
    outer_next, momentum_next, local_next = fragment(
        total, outer_params, outer_momentum, snapshot[0], local_params[0], due_rows, replicas
    )
    xlt, dr = early(parts[:-1], left, right)
    update, first_next, second_next = finish(
        parts[-1], xlt, dr, left, right, first_moment[0, 0], second_moment[0, 0]
    )
    return (
        update[None, None],
        first_next[None, None],
        second_next[None, None],
        outer_next,
        momentum_next,
        local_next[None],
    )


def solution(mesh):
    return jax.shard_map(
        per_device,
        mesh=mesh,
        in_specs=(
            P(("replica", "fsdp"), None),
            P(("replica", "fsdp"), None),
            P(),
            P("replica", "fsdp", None, None),
            P("replica", "fsdp", None, None),
            P("replica", "fsdp", None, None),
            P("replica", "fsdp", None, None),
            P("fsdp", None),
            P("fsdp", None),
            P("replica", "fsdp", None),
            P("replica", "fsdp", None),
            P("fsdp"),
        ),
        out_specs=(
            P("replica", "fsdp", None, None),
            P("replica", "fsdp", None, None),
            P("replica", "fsdp", None, None),
            P("fsdp", None),
            P("fsdp", None),
            P("replica", "fsdp", None),
        ),
        check_vma=False,
    )
```

```python
import functools

import jax
import jax.numpy as jnp
from jax import lax
from jax.experimental import pallas as pl
from jax.experimental.pallas import tpu as pltpu
from jax.sharding import PartitionSpec as P

MIB = 1 << 20
CORES = 2
CORRECT = 1.0 - 0.95**10


def any_spec():
    return pl.BlockSpec(memory_space=pl.ANY)


def hbm_spec():
    return pl.BlockSpec(memory_space=pltpu.HBM)


def vmem_spec():
    return pl.BlockSpec(memory_space=pltpu.VMEM)


def gather_kernel(n, width, columns, order, ids, tokens, out_grads, *refs):
    outs, sems = refs[:n], refs[n]
    me = lax.axis_index("fsdp")
    copies = []
    for k, shift in enumerate(order):
        block = ids[lax.rem(me + shift, n)]
        row = pl.multiple_of(block // columns * width, width)
        col = pl.multiple_of(lax.rem(block, columns) * width, width)
        copies.append(
            pltpu.make_async_copy(tokens.at[:, pl.ds(row, width)], outs[k].at[0], sems.at[0, k])
        )
        copies.append(
            pltpu.make_async_copy(out_grads.at[:, pl.ds(col, width)], outs[k].at[1], sems.at[1, k])
        )
    for copy in copies:
        copy.start()
    for copy in copies:
        copy.wait()


def gather(tokens, out_grads, block_ids, width, n, order):
    rows = tokens.shape[0]
    return pl.pallas_call(
        functools.partial(gather_kernel, n, width, out_grads.shape[1] // width, order),
        out_shape=[jax.ShapeDtypeStruct((2, rows, width), tokens.dtype)] * n,
        in_specs=[pl.BlockSpec(memory_space=pltpu.SMEM), hbm_spec(), hbm_spec()],
        out_specs=[any_spec()] * n,
        scratch_shapes=[pltpu.SemaphoreType.DMA((2, n))],
        compiler_params=pltpu.CompilerParams(vmem_limit_bytes=60 * MIB),
        cost_estimate=pl.CostEstimate(flops=0, bytes_accessed=16 * n * rows * width, transcendentals=0),
        name="gather_slots",
    )(block_ids, tokens, out_grads)


def sum_kernel(
    chips, own, out, sib, part, inbox, s1, r1, s2, r2, s3, r3, s4, r4
):
    me = lax.axis_index("replica")
    chip, core = me // CORES, lax.rem(me, CORES)
    half, wide = own.shape[0] // CORES, own.shape[1] // chips
    other = 1 - core
    sibling = {"replica": chip * CORES + other}

    def peer(k):
        return lax.rem(chip + k, chips)

    def rows(c):
        return pl.ds(pl.multiple_of(c * half, half), half)

    def cols(c):
        return pl.ds(pl.multiple_of(c * wide, wide), wide)

    def to(k):
        return {"replica": peer(k) * CORES + core}

    barrier = pltpu.get_barrier_semaphore()
    pl.semaphore_signal(barrier, inc=1, device_id=sibling, device_id_type=pl.DeviceIdType.MESH)
    for k in range(1, chips):
        pl.semaphore_signal(barrier, inc=1, device_id=to(k), device_id_type=pl.DeviceIdType.MESH)
    pl.semaphore_wait(barrier, chips)

    turns = list(range(1, chips)) + [0]
    remote = functools.partial(
        pltpu.make_async_remote_copy, device_id_type=pl.DeviceIdType.MESH
    )
    first = {
        k: remote(own.at[rows(other), cols(peer(k))], sib.at[k], s1.at[k], r1.at[k], device_id=sibling)
        for k in turns
    }
    for k in turns:
        first[k].start()
    second = {}
    for k in turns:
        first[k].wait_recv()
        pair = own[rows(core), cols(peer(k))].astype(jnp.float32) + sib[k].astype(jnp.float32)
        if k:
            part[k] = pair.astype(part.dtype)
            second[k] = remote(part.at[k], inbox.at[k], s2.at[k], r2.at[k], device_id=to(k))
            second[k].start()
        else:
            part[0] = pair.astype(part.dtype)
    for k in range(1, chips):
        second[k].wait_recv()
    total = part[0].astype(jnp.float32)
    for k in range(1, chips):
        total = total + inbox[k].astype(jnp.float32)
    out[rows(core), cols(chip)] = total.astype(out.dtype)

    mine = out.at[rows(core), cols(chip)]
    third = {}
    for k in range(1, chips):
        third[k] = remote(mine, mine, s3.at[k], r3.at[k], device_id=to(k))
        third[k].start()
    fourth = {0: remote(mine, mine, s4.at[0], r4.at[0], device_id=sibling)}
    fourth[0].start()
    for k in range(1, chips):
        third[k].wait_recv()
        landed = out.at[rows(core), cols(lax.rem(chip + chips - k, chips))]
        fourth[k] = remote(landed, landed, s4.at[k], r4.at[k], device_id=sibling)
        fourth[k].start()
    for k in range(chips):
        fourth[k].wait_recv()
        fourth[k].wait_send()
        first[k].wait_send()
        if k:
            second[k].wait_send()
            third[k].wait_send()


def replica_sum(snap, replicas):
    chips = replicas // CORES
    rows, cols = snap.shape
    piece = (chips, rows // CORES, cols // chips)
    dma = pltpu.SemaphoreType.DMA((chips,))
    return pl.pallas_call(
        functools.partial(sum_kernel, chips),
        out_shape=jax.ShapeDtypeStruct(snap.shape, snap.dtype),
        in_specs=[vmem_spec()],
        out_specs=vmem_spec(),
        scratch_shapes=[pltpu.VMEM(piece, snap.dtype)] * 3 + [dma] * 8,
        compiler_params=pltpu.CompilerParams(
            collective_id=0, has_side_effects=True, vmem_limit_bytes=16 * MIB
        ),
        cost_estimate=pl.CostEstimate(flops=0, bytes_accessed=100 * snap.size, transcendentals=0),
        name="replica_sum",
    )(snap)


def fragment_kernel(
    step, scale, total, outer, momentum, snap, local, due, outer_next, momentum_next, local_next,
    outer_out, momentum_out, local_out, sems,
):
    stores = []
    for k in range(outer.shape[0] // step):
        r = slice(k * step, (k + 1) * step)
        base, old = outer[r, :], momentum[r, :]
        pseudo = base - total[r, :].astype(jnp.float32) * scale
        moment = 0.9 * old + pseudo
        stepped = base - 0.7 * (pseudo + 0.9 * moment)
        keep = due[r, :] == 1
        outer_out[r, :] = jnp.where(keep, stepped, base)
        momentum_out[r, :] = jnp.where(keep, moment, old)
        here = local[r, :].astype(jnp.float32)
        merged = stepped + (here - snap[r, :].astype(jnp.float32))
        local_out[r, :] = jnp.where(keep, merged, here).astype(local_out.dtype)
        for m, (src, dst) in enumerate(
            ((outer_out, outer_next), (momentum_out, momentum_next), (local_out, local_next))
        ):
            stores.append(pltpu.make_async_copy(src.at[r], dst.at[r], sems.at[m, k]))
            stores[-1].start()
    for copy in stores:
        copy.wait()


def fragment(total, outer, momentum, snap, local, due, replicas):
    rows, cols = outer.shape
    step = 16
    return pl.pallas_call(
        functools.partial(fragment_kernel, step, 1.0 / replicas),
        out_shape=[
            jax.ShapeDtypeStruct(outer.shape, outer.dtype),
            jax.ShapeDtypeStruct(outer.shape, outer.dtype),
            jax.ShapeDtypeStruct(local.shape, local.dtype),
        ],
        in_specs=[vmem_spec()] * 6,
        out_specs=[hbm_spec()] * 3,
        scratch_shapes=[
            pltpu.VMEM(outer.shape, outer.dtype),
            pltpu.VMEM(outer.shape, outer.dtype),
            pltpu.VMEM(local.shape, local.dtype),
            pltpu.SemaphoreType.DMA((3, rows // step)),
        ],
        compiler_params=pltpu.CompilerParams(vmem_limit_bytes=16 * MIB),
        cost_estimate=pl.CostEstimate(
            flops=12 * outer.size, bytes_accessed=16 * outer.size, transcendentals=0
        ),
        name="fragment_step",
    )(total, outer, momentum, snap, local, due.reshape(rows, 1))


def early_kernel(m, *refs):
    parts, left, right, xlt, dr = refs[:m], refs[m], refs[m + 1], refs[m + 2], refs[m + 3]
    rows = parts[0].shape[1]
    for k in range(m):
        span = slice(k * rows, (k + 1) * rows)
        xl = jnp.dot(parts[k][0], left[...], preferred_element_type=jnp.float32)
        xlt[:, span] = xl.T.astype(xlt.dtype)
        dr[span, :] = jnp.dot(
            parts[k][1], right[...], preferred_element_type=jnp.float32
        ).astype(dr.dtype)


def early(parts, left, right):
    m = len(parts)
    rows, width = parts[0].shape[1:]
    return pl.pallas_call(
        functools.partial(early_kernel, m),
        out_shape=[
            jax.ShapeDtypeStruct((width, m * rows), left.dtype),
            jax.ShapeDtypeStruct((m * rows, width), left.dtype),
        ],
        in_specs=[vmem_spec()] * (m + 2),
        out_specs=[vmem_spec()] * 2,
        compiler_params=pltpu.CompilerParams(vmem_limit_bytes=16 * MIB),
        cost_estimate=pl.CostEstimate(
            flops=4 * m * rows * width * width, bytes_accessed=8 * MIB, transcendentals=0
        ),
        name="early_products",
    )(*parts, left, right)


def tail_kernel(step, m, *refs):
    parts = refs[:m]
    (
        xlt_in, dr_in, left, right, first, second, update, first_next, second_next,
        xlt, dr, first_out, second_out, back, up, sems,
    ) = refs[m:]
    done = dr_in.shape[0]
    chunks = [slice(k * step, (k + 1) * step) for k in range(left.shape[0] // step)]
    xl = jnp.dot(
        jnp.concatenate([part[0] for part in parts]),
        left[...],
        preferred_element_type=jnp.float32,
    )
    xlt[:, :done] = xlt_in[...]
    xlt[:, done:] = xl.T.astype(xlt.dtype)
    dr[:done, :] = dr_in[...]
    grads = jnp.concatenate([part[1] for part in parts])

    def rotate(c):
        dr[done:, c] = jnp.dot(
            grads, right[:, c], preferred_element_type=jnp.float32
        ).astype(dr.dtype)
        return jnp.dot(xlt[...], dr[:, c], preferred_element_type=jnp.float32)

    stores = []

    def store(src, dst, c, which, k):
        stores.append(pltpu.make_async_copy(src.at[:, c], dst.at[:, c], sems.at[which, k]))
        stores[-1].start()

    ahead = rotate(chunks[0])
    for k, c in enumerate(chunks):
        rotated = ahead
        if k + 1 < len(chunks):
            ahead = rotate(chunks[k + 1])
        one = 0.95 * first[:, c].astype(jnp.float32) + 0.05 * rotated
        two = 0.95 * second[:, c].astype(jnp.float32) + 0.05 * (rotated * rotated)
        first_out[:, c] = one.astype(first_out.dtype)
        second_out[:, c] = two.astype(second_out.dtype)
        scaled = CORRECT * two
        bottom = scaled * lax.rsqrt(scaled) + CORRECT * 1e-08
        guess = pl.reciprocal(bottom, approx=True)
        direction = (one * (guess * (2.0 - bottom * guess))).astype(jnp.bfloat16)
        back[:, c] = jnp.dot(left[...], direction, preferred_element_type=jnp.float32).astype(
            back.dtype
        )
        store(first_out, first_next, c, 0, k)
        store(second_out, second_next, c, 1, k)
    for k, c in enumerate(chunks):
        up[:, c] = lax.dot_general(
            back[...], right[c, :], (((1,), (1,)), ((), ())), preferred_element_type=jnp.float32
        ).astype(up.dtype)
        store(up, update, c, 2, k)
    for copy in stores:
        copy.wait()


def finish(parts, xlt, dr, left, right, first, second):
    m = len(parts)
    width = left.shape[0]
    rows = parts[0].shape[1]
    tokens = dr.shape[0] + m * rows
    step = 256
    square = pltpu.VMEM((width, width), left.dtype)
    return pl.pallas_call(
        functools.partial(tail_kernel, step, m),
        out_shape=[jax.ShapeDtypeStruct((width, width), left.dtype)] * 3,
        in_specs=[vmem_spec()] * (m + 6),
        out_specs=[hbm_spec()] * 3,
        scratch_shapes=[
            pltpu.VMEM((width, tokens), left.dtype),
            pltpu.VMEM((tokens, width), left.dtype),
        ]
        + [square] * 4
        + [pltpu.SemaphoreType.DMA((3, width // step))],
        compiler_params=pltpu.CompilerParams(vmem_limit_bytes=32 * MIB),
        cost_estimate=pl.CostEstimate(
            flops=6 * width**3, bytes_accessed=14 * MIB, transcendentals=2 * width * width
        ),
        name="soap_tail",
    )(*parts, xlt, dr, left, right, first, second)


def per_device(
    tokens,
    out_grads,
    block_ids,
    left_basis,
    right_basis,
    first_moment,
    second_moment,
    outer_params,
    outer_momentum,
    snapshot,
    local_params,
    due_rows,
):
    n = lax.axis_size("fsdp")
    replicas = lax.axis_size("replica")
    left, right = left_basis[0, 0], right_basis[0, 0]
    order = [0] + sorted(range(1, n), key=lambda s: abs(2 * s - n))
    sent = gather(tokens, out_grads, block_ids, left.shape[-1], n, order)
    parts = [sent[0]]
    for k in range(1, n):
        pairs = [(i, (i + order[k]) % n) for i in range(n)]
        parts.append(lax.ppermute(sent[k], "fsdp", pairs))
    total = replica_sum(snapshot[0], replicas)
    outer_next, momentum_next, local_next = fragment(
        total, outer_params, outer_momentum, snapshot[0], local_params[0], due_rows, replicas
    )
    xlt, dr = early(parts[: n // 2], left, right)
    update, first_next, second_next = finish(
        parts[n // 2 :], xlt, dr, left, right, first_moment[0, 0], second_moment[0, 0]
    )
    return (
        update[None, None],
        first_next[None, None],
        second_next[None, None],
        outer_next,
        momentum_next,
        local_next[None],
    )


def solution(mesh):
    return jax.shard_map(
        per_device,
        mesh=mesh,
        in_specs=(
            P(("replica", "fsdp"), None),
            P(("replica", "fsdp"), None),
            P(),
            P("replica", "fsdp", None, None),
            P("replica", "fsdp", None, None),
            P("replica", "fsdp", None, None),
            P("replica", "fsdp", None, None),
            P("fsdp", None),
            P("fsdp", None),
            P("replica", "fsdp", None),
            P("replica", "fsdp", None),
            P("fsdp"),
        ),
        out_specs=(
            P("replica", "fsdp", None, None),
            P("replica", "fsdp", None, None),
            P("replica", "fsdp", None, None),
            P("fsdp", None),
            P("fsdp", None),
            P("replica", "fsdp", None),
        ),
        check_vma=False,
    )
```

```python
import functools

import jax
import jax.numpy as jnp
from jax import lax
from jax.experimental import pallas as pl
from jax.experimental.pallas import tpu as pltpu
from jax.sharding import PartitionSpec as P

MIB = 1 << 20
CORES = 2
CORRECT = 1.0 - 0.95**10


def any_spec():
    return pl.BlockSpec(memory_space=pl.ANY)


def hbm_spec():
    return pl.BlockSpec(memory_space=pltpu.HBM)


def vmem_spec():
    return pl.BlockSpec(memory_space=pltpu.VMEM)


def gather_kernel(n, width, columns, order, ids, tokens, out_grads, *refs):
    outs, sems = refs[:n], refs[n]
    me = lax.axis_index("fsdp")
    copies = []
    for k, shift in enumerate(order):
        block = ids[lax.rem(me + shift, n)]
        row = pl.multiple_of(block // columns * width, width)
        col = pl.multiple_of(lax.rem(block, columns) * width, width)
        copies.append(
            pltpu.make_async_copy(tokens.at[:, pl.ds(row, width)], outs[k].at[0], sems.at[0, k])
        )
        copies.append(
            pltpu.make_async_copy(out_grads.at[:, pl.ds(col, width)], outs[k].at[1], sems.at[1, k])
        )
    for copy in copies:
        copy.start()
    for copy in copies:
        copy.wait()


def gather(tokens, out_grads, block_ids, width, n, order):
    rows = tokens.shape[0]
    return pl.pallas_call(
        functools.partial(gather_kernel, n, width, out_grads.shape[1] // width, order),
        out_shape=[jax.ShapeDtypeStruct((2, rows, width), tokens.dtype)] * n,
        in_specs=[pl.BlockSpec(memory_space=pltpu.SMEM), hbm_spec(), hbm_spec()],
        out_specs=[vmem_spec()] * n,
        scratch_shapes=[pltpu.SemaphoreType.DMA((2, n))],
        compiler_params=pltpu.CompilerParams(vmem_limit_bytes=60 * MIB),
        cost_estimate=pl.CostEstimate(flops=0, bytes_accessed=16 * n * rows * width, transcendentals=0),
        name="gather_slots",
    )(block_ids, tokens, out_grads)


def sum_kernel(
    chips, own, outer, momentum, local, out, outer_here, momentum_here, local_here,
    sib, part, inbox, s1, r1, s2, r2, s3, r3, s4, r4, sems,
):
    loads = [
        pltpu.make_async_copy(src, dst, sems.at[k])
        for k, (src, dst) in enumerate(
            ((outer, outer_here), (momentum, momentum_here), (local, local_here))
        )
    ]
    for copy in loads:
        copy.start()
    me = lax.axis_index("replica")
    chip, core = me // CORES, lax.rem(me, CORES)
    half, wide = own.shape[0] // CORES, own.shape[1] // chips
    other = 1 - core
    sibling = {"replica": chip * CORES + other}

    def peer(k):
        return lax.rem(chip + k, chips)

    def rows(c):
        return pl.ds(pl.multiple_of(c * half, half), half)

    def cols(c):
        return pl.ds(pl.multiple_of(c * wide, wide), wide)

    def to(k):
        return {"replica": peer(k) * CORES + core}

    barrier = pltpu.get_barrier_semaphore()
    pl.semaphore_signal(barrier, inc=1, device_id=sibling, device_id_type=pl.DeviceIdType.MESH)
    for k in range(1, chips):
        pl.semaphore_signal(barrier, inc=1, device_id=to(k), device_id_type=pl.DeviceIdType.MESH)
    pl.semaphore_wait(barrier, chips)

    turns = list(range(1, chips)) + [0]
    remote = functools.partial(
        pltpu.make_async_remote_copy, device_id_type=pl.DeviceIdType.MESH
    )
    first = {
        k: remote(own.at[rows(other), cols(peer(k))], sib.at[k], s1.at[k], r1.at[k], device_id=sibling)
        for k in turns
    }
    for k in turns:
        first[k].start()
    second = {}
    for k in turns:
        first[k].wait_recv()
        pair = own[rows(core), cols(peer(k))].astype(jnp.float32) + sib[k].astype(jnp.float32)
        if k:
            part[k] = pair.astype(part.dtype)
            second[k] = remote(part.at[k], inbox.at[k], s2.at[k], r2.at[k], device_id=to(k))
            second[k].start()
        else:
            part[0] = pair.astype(part.dtype)
    for k in range(1, chips):
        second[k].wait_recv()
    total = part[0].astype(jnp.float32)
    for k in range(1, chips):
        total = total + inbox[k].astype(jnp.float32)
    out[rows(core), cols(chip)] = total.astype(out.dtype)

    mine = out.at[rows(core), cols(chip)]
    third = {}
    for k in range(1, chips):
        third[k] = remote(mine, mine, s3.at[k], r3.at[k], device_id=to(k))
        third[k].start()
    fourth = {0: remote(mine, mine, s4.at[0], r4.at[0], device_id=sibling)}
    fourth[0].start()
    for k in range(1, chips):
        third[k].wait_recv()
        landed = out.at[rows(core), cols(lax.rem(chip + chips - k, chips))]
        fourth[k] = remote(landed, landed, s4.at[k], r4.at[k], device_id=sibling)
        fourth[k].start()
    for k in range(chips):
        fourth[k].wait_recv()
        fourth[k].wait_send()
        first[k].wait_send()
        if k:
            second[k].wait_send()
            third[k].wait_send()
    for copy in loads:
        copy.wait()


def replica_sum(snap, outer, momentum, local, replicas):
    chips = replicas // CORES
    rows, cols = snap.shape
    piece = (chips, rows // CORES, cols // chips)
    dma = pltpu.SemaphoreType.DMA((chips,))
    return pl.pallas_call(
        functools.partial(sum_kernel, chips),
        out_shape=[
            jax.ShapeDtypeStruct(x.shape, x.dtype) for x in (snap, outer, momentum, local)
        ],
        in_specs=[vmem_spec()] + [hbm_spec()] * 3,
        out_specs=[vmem_spec()] * 4,
        scratch_shapes=[pltpu.VMEM(piece, snap.dtype)] * 3
        + [dma] * 8
        + [pltpu.SemaphoreType.DMA((3,))],
        compiler_params=pltpu.CompilerParams(
            collective_id=0, has_side_effects=True, vmem_limit_bytes=36 * MIB
        ),
        cost_estimate=pl.CostEstimate(flops=0, bytes_accessed=100 * snap.size, transcendentals=0),
        name="replica_sum",
    )(snap, outer, momentum, local)


def fragment_kernel(
    step, scale, total, outer, momentum, snap, local, due, outer_next, momentum_next, local_next,
    outer_out, momentum_out, local_out, sems,
):
    stores = []
    for k in range(outer.shape[0] // step):
        r = slice(k * step, (k + 1) * step)
        base, old = outer[r, :], momentum[r, :]
        pseudo = base - total[r, :].astype(jnp.float32) * scale
        moment = 0.9 * old + pseudo
        stepped = base - 0.7 * (pseudo + 0.9 * moment)
        keep = due[r, :] == 1
        outer_out[r, :] = jnp.where(keep, stepped, base)
        momentum_out[r, :] = jnp.where(keep, moment, old)
        here = local[r, :].astype(jnp.float32)
        merged = stepped + (here - snap[r, :].astype(jnp.float32))
        local_out[r, :] = jnp.where(keep, merged, here).astype(local_out.dtype)
        for m, (src, dst) in enumerate(
            ((outer_out, outer_next), (momentum_out, momentum_next), (local_out, local_next))
        ):
            stores.append(pltpu.make_async_copy(src.at[r], dst.at[r], sems.at[m, k]))
            stores[-1].start()
    for copy in stores:
        copy.wait()


def fragment(total, outer, momentum, snap, local, due, replicas):
    rows, cols = outer.shape
    step = 16
    return pl.pallas_call(
        functools.partial(fragment_kernel, step, 1.0 / replicas),
        out_shape=[
            jax.ShapeDtypeStruct(outer.shape, outer.dtype),
            jax.ShapeDtypeStruct(outer.shape, outer.dtype),
            jax.ShapeDtypeStruct(local.shape, local.dtype),
        ],
        in_specs=[vmem_spec()] * 6,
        out_specs=[hbm_spec()] * 3,
        scratch_shapes=[
            pltpu.VMEM(outer.shape, outer.dtype),
            pltpu.VMEM(outer.shape, outer.dtype),
            pltpu.VMEM(local.shape, local.dtype),
            pltpu.SemaphoreType.DMA((3, rows // step)),
        ],
        compiler_params=pltpu.CompilerParams(vmem_limit_bytes=16 * MIB),
        cost_estimate=pl.CostEstimate(
            flops=12 * outer.size, bytes_accessed=16 * outer.size, transcendentals=0
        ),
        name="fragment_step",
    )(total, outer, momentum, snap, local, due.reshape(rows, 1))


def early_kernel(m, *refs):
    parts, left, right, xlt, dr = refs[:m], refs[m], refs[m + 1], refs[m + 2], refs[m + 3]
    rows = parts[0].shape[1]
    for k in range(m):
        span = slice(k * rows, (k + 1) * rows)
        xl = jnp.dot(parts[k][0], left[...], preferred_element_type=jnp.float32)
        xlt[:, span] = xl.T.astype(xlt.dtype)
        dr[span, :] = jnp.dot(
            parts[k][1], right[...], preferred_element_type=jnp.float32
        ).astype(dr.dtype)


def early(parts, left, right):
    m = len(parts)
    rows, width = parts[0].shape[1:]
    return pl.pallas_call(
        functools.partial(early_kernel, m),
        out_shape=[
            jax.ShapeDtypeStruct((width, m * rows), left.dtype),
            jax.ShapeDtypeStruct((m * rows, width), left.dtype),
        ],
        in_specs=[vmem_spec()] * (m + 2),
        out_specs=[vmem_spec()] * 2,
        compiler_params=pltpu.CompilerParams(vmem_limit_bytes=16 * MIB),
        cost_estimate=pl.CostEstimate(
            flops=4 * m * rows * width * width, bytes_accessed=8 * MIB, transcendentals=0
        ),
        name="early_products",
    )(*parts, left, right)


def tail_kernel(step, m, *refs):
    parts = refs[:m]
    (
        xlt_in, dr_in, left, right, first, second, update, first_next, second_next,
        xlt, dr, first_out, second_out, back, up, sems,
    ) = refs[m:]
    done = dr_in.shape[0]
    chunks = [slice(k * step, (k + 1) * step) for k in range(left.shape[0] // step)]
    xl = jnp.dot(
        jnp.concatenate([part[0] for part in parts]),
        left[...],
        preferred_element_type=jnp.float32,
    )
    xlt[:, :done] = xlt_in[...]
    xlt[:, done:] = xl.T.astype(xlt.dtype)
    dr[:done, :] = dr_in[...]
    grads = jnp.concatenate([part[1] for part in parts])

    def rotate(c):
        dr[done:, c] = jnp.dot(
            grads, right[:, c], preferred_element_type=jnp.float32
        ).astype(dr.dtype)
        return jnp.dot(xlt[...], dr[:, c], preferred_element_type=jnp.float32)

    stores = []

    def store(src, dst, c, which, k):
        stores.append(pltpu.make_async_copy(src.at[:, c], dst.at[:, c], sems.at[which, k]))
        stores[-1].start()

    ahead = rotate(chunks[0])
    for k, c in enumerate(chunks):
        rotated = ahead
        if k + 1 < len(chunks):
            ahead = rotate(chunks[k + 1])
        one = 0.95 * first[:, c].astype(jnp.float32) + 0.05 * rotated
        two = 0.95 * second[:, c].astype(jnp.float32) + 0.05 * (rotated * rotated)
        first_out[:, c] = one.astype(first_out.dtype)
        second_out[:, c] = two.astype(second_out.dtype)
        scaled = CORRECT * two
        bottom = scaled * lax.rsqrt(scaled) + CORRECT * 1e-08
        guess = pl.reciprocal(bottom, approx=True)
        direction = (one * (guess * (2.0 - bottom * guess))).astype(jnp.bfloat16)
        back[:, c] = jnp.dot(left[...], direction, preferred_element_type=jnp.float32).astype(
            back.dtype
        )
        store(first_out, first_next, c, 0, k)
        store(second_out, second_next, c, 1, k)
    for k, c in enumerate(chunks):
        up[:, c] = lax.dot_general(
            back[...], right[c, :], (((1,), (1,)), ((), ())), preferred_element_type=jnp.float32
        ).astype(up.dtype)
        store(up, update, c, 2, k)
    for copy in stores:
        copy.wait()


def finish(parts, xlt, dr, left, right, first, second):
    m = len(parts)
    width = left.shape[0]
    rows = parts[0].shape[1]
    tokens = dr.shape[0] + m * rows
    step = 256
    square = pltpu.VMEM((width, width), left.dtype)
    return pl.pallas_call(
        functools.partial(tail_kernel, step, m),
        out_shape=[jax.ShapeDtypeStruct((width, width), left.dtype)] * 3,
        in_specs=[vmem_spec()] * (m + 6),
        out_specs=[hbm_spec()] * 3,
        scratch_shapes=[
            pltpu.VMEM((width, tokens), left.dtype),
            pltpu.VMEM((tokens, width), left.dtype),
        ]
        + [square] * 4
        + [pltpu.SemaphoreType.DMA((3, width // step))],
        compiler_params=pltpu.CompilerParams(vmem_limit_bytes=32 * MIB),
        cost_estimate=pl.CostEstimate(
            flops=6 * width**3, bytes_accessed=14 * MIB, transcendentals=2 * width * width
        ),
        name="soap_tail",
    )(*parts, xlt, dr, left, right, first, second)


def per_device(
    tokens,
    out_grads,
    block_ids,
    left_basis,
    right_basis,
    first_moment,
    second_moment,
    outer_params,
    outer_momentum,
    snapshot,
    local_params,
    due_rows,
):
    n = lax.axis_size("fsdp")
    replicas = lax.axis_size("replica")
    left, right = left_basis[0, 0], right_basis[0, 0]
    order = [0] + sorted(range(1, n), key=lambda s: abs(2 * s - n))
    sent = gather(tokens, out_grads, block_ids, left.shape[-1], n, order)
    parts = [sent[0]]
    for k in range(1, n):
        pairs = [(i, (i + order[k]) % n) for i in range(n)]
        parts.append(lax.ppermute(sent[k], "fsdp", pairs))
    total, outer, momentum, local = replica_sum(
        snapshot[0], outer_params, outer_momentum, local_params[0], replicas
    )
    outer_next, momentum_next, local_next = fragment(
        total, outer, momentum, snapshot[0], local, due_rows, replicas
    )
    xlt, dr = early(parts[: n // 2], left, right)
    update, first_next, second_next = finish(
        parts[n // 2 :], xlt, dr, left, right, first_moment[0, 0], second_moment[0, 0]
    )
    return (
        update[None, None],
        first_next[None, None],
        second_next[None, None],
        outer_next,
        momentum_next,
        local_next[None],
    )


def solution(mesh):
    return jax.shard_map(
        per_device,
        mesh=mesh,
        in_specs=(
            P(("replica", "fsdp"), None),
            P(("replica", "fsdp"), None),
            P(),
            P("replica", "fsdp", None, None),
            P("replica", "fsdp", None, None),
            P("replica", "fsdp", None, None),
            P("replica", "fsdp", None, None),
            P("fsdp", None),
            P("fsdp", None),
            P("replica", "fsdp", None),
            P("replica", "fsdp", None),
            P("fsdp"),
        ),
        out_specs=(
            P("replica", "fsdp", None, None),
            P("replica", "fsdp", None, None),
            P("replica", "fsdp", None, None),
            P("fsdp", None),
            P("fsdp", None),
            P("replica", "fsdp", None),
        ),
        check_vma=False,
    )
```
